256 devices in a mesh: dp: 16 (over z, core), sp: 16 (over x, y).
Axes of the slice: x: 4, y: 4, z: 8, core: 2. Of those that a mesh axis runs over, the one named last changes fastest.
Arguments:
- layer_input: bfloat16 [32768, 4096], P(('dp', 'sp')), may hold values from -24 to 24
- queries: bfloat16 [32768, 4096], P(('dp', 'sp')), may hold values from -36 to 36
- keys: bfloat16 [32768, 256], P(('dp', 'sp')), may hold values from -4 to 4
- values: bfloat16 [32768, 256], P(('dp', 'sp')), may hold values from -6 to 6
- out_grad: bfloat16 [32768, 4096], P(('dp', 'sp')), may hold values from -3 to 3
- key_value_weight: bfloat16 [4096, 512], P(('dp', 'sp')), may hold values from -0.09375 to 0.09375
Outputs:
- query_grad: bfloat16 [32768, 4096], P(('dp', 'sp'))
- input_grad: bfloat16 [32768, 4096], P(('dp', 'sp'))
- weight_grad: float32 [4096, 512], P(('dp', 'sp'))
The draws below stay inside these ranges and needn't reach their ends.
All inputs are finite; a program needn't handle non-finite values.
Results may differ from the reference program's by a relative error of at most 0.015.
Values may be sent and summed in bfloat16 or wider, within the bound.
A program may use at most 128 MiB of HBM per device.

```python
import jax
import jax.numpy as jnp
from jax import lax

MODEL_WIDTH = 4096
QUERY_HEADS = 32
KEY_VALUE_HEADS = 2
HEAD_SIZE = 128
SEQUENCE_TOKENS = 2048
ALL_TOKENS = 32768
N_DP = 16
N_SP = 16


def key_table(key):
    normal_key = jax.random.fold_in(key, 11)
    key_value_table_shape = (ALL_TOKENS, KEY_VALUE_HEADS * HEAD_SIZE)
    normal_part = jnp.clip(jax.random.normal(normal_key, key_value_table_shape, jnp.float32), -4.0, 4.0)
    return normal_part


def draw_keys(key, part):
    return key_table(key).astype(jnp.bfloat16)


def draw_queries(key, part):
    own_key = jax.random.fold_in(key, 2)
    return jnp.clip(jax.random.normal(own_key, (ALL_TOKENS, QUERY_HEADS * HEAD_SIZE), jnp.float32), -4.0, 4.0).astype(jnp.bfloat16)


def strengthened(values, rng, source, target, blocks, factor):
    def block_of(dim):
        return (jnp.arange(values.shape[dim]) // (values.shape[dim] // blocks)).reshape((-1,) + (1,) * (values.ndim - 1 - dim))

    first = jax.random.permutation(rng, blocks)[block_of(target)]
    second = (block_of(target) + blocks // 2) % blocks
    return jnp.where((block_of(source) == first) | (block_of(source) == second), factor * values, values)


def level_of(key, shape, cuts, low, largest):
    level = 1.0
    for axis_at, blocks in cuts:
        steps = jax.random.uniform(jax.random.fold_in(jax.random.fold_in(key, 6), axis_at), (blocks,), jnp.float32, low / len(cuts), largest / len(cuts))
        level = level * jnp.repeat(jnp.exp(steps), shape[axis_at] // blocks).reshape((-1,) + (1,) * (len(shape) - 1 - axis_at))
    return level


def bell_draw(stream_key, shape, width, most, pieces=(), kind=jnp.bfloat16):
    drawn = width * jax.random.normal(stream_key, shape, jnp.float32)
    if pieces:
        drawn = drawn * level_of(stream_key, shape, pieces, -0.22, 0.18)
    return jnp.clip(drawn, -most, most).astype(kind)


def noise_with(key, shape, width, limit, split, heavy, kind=jnp.bfloat16):
    drawn = width * jax.random.normal(key, shape, jnp.float32)
    if split:
        drawn = drawn * level_of(key, shape, split, -0.22, 0.18)
    return jnp.clip(strengthened(drawn, jax.random.fold_in(key, 3), *heavy), -limit, limit).astype(kind)


def setup_inputs(seed: int = 0) -> dict:
    streams_of = jax.random.split(jax.random.key(seed), 7)
    return {
        "layer_input": noise_with(streams_of[0], (ALL_TOKENS, MODEL_WIDTH), 1.0, 24.0, ((0, 256),), (0, 1, 256, 6.0)),
        "queries": draw_queries(jax.random.fold_in(streams_of[6], 71), 0),
        "keys": draw_keys(jax.random.fold_in(streams_of[6], 71), 0),
        "values": bell_draw(streams_of[3], (ALL_TOKENS, KEY_VALUE_HEADS * HEAD_SIZE), 1.0, 6.0, ((0, 256),)),
        "out_grad": bell_draw(streams_of[4], (ALL_TOKENS, QUERY_HEADS * HEAD_SIZE), 0.5, 3.0, ((0, 256),)),
        "key_value_weight": bell_draw(streams_of[5], (MODEL_WIDTH, 2 * KEY_VALUE_HEADS * HEAD_SIZE), MODEL_WIDTH ** -0.5, 0.09375, ((0, 256),)),
    }


def group_grads(queries, keys, values, out_grad, flat_index):
    local_heads = QUERY_HEADS // N_SP
    seq_index = flat_index // N_SP
    query_head_group = flat_index % N_SP
    key_value_head = query_head_group // (N_SP // KEY_VALUE_HEADS)
    row_start = (seq_index * SEQUENCE_TOKENS).astype(jnp.int32)
    query_col = (query_head_group * (local_heads * HEAD_SIZE)).astype(jnp.int32)
    key_col = (key_value_head * HEAD_SIZE).astype(jnp.int32)
    score_scale = HEAD_SIZE ** -0.5
    q_part = lax.dynamic_slice(queries, (row_start, query_col), (SEQUENCE_TOKENS, local_heads * HEAD_SIZE))
    g_part = lax.dynamic_slice(out_grad, (row_start, query_col), (SEQUENCE_TOKENS, local_heads * HEAD_SIZE))
    k_part = lax.dynamic_slice(keys, (row_start, key_col), (SEQUENCE_TOKENS, HEAD_SIZE)).astype(jnp.float32)
    v_part = lax.dynamic_slice(values, (row_start, key_col), (SEQUENCE_TOKENS, HEAD_SIZE)).astype(jnp.float32)
    q_part = q_part.reshape(SEQUENCE_TOKENS, local_heads, HEAD_SIZE).astype(jnp.float32)
    g_part = g_part.reshape(SEQUENCE_TOKENS, local_heads, HEAD_SIZE).astype(jnp.float32)
    scores = jnp.einsum("qhd,kd->hqk", q_part, k_part) * score_scale
    visible = jnp.tril(jnp.ones((SEQUENCE_TOKENS, SEQUENCE_TOKENS), dtype=bool))
    scores = jnp.where(visible[None], scores, -jnp.inf)
    row_max = jnp.max(scores, axis=-1, keepdims=True)
    log_total = row_max + jnp.log(jnp.sum(jnp.exp(scores - row_max), axis=-1, keepdims=True))
    probs = jnp.exp(scores - log_total)
    dprobs = jnp.einsum("qhd,kd->hqk", g_part, v_part)
    row_dot = jnp.sum(probs * dprobs, axis=-1, keepdims=True)
    prob_low = lax.optimization_barrier(probs.astype(jnp.bfloat16)).astype(jnp.float32)
    dscore_low = lax.optimization_barrier((probs * (dprobs - row_dot)).astype(jnp.bfloat16)).astype(jnp.float32)
    dq_part = (jnp.einsum("hqk,kd->qhd", dscore_low, k_part) * score_scale).astype(jnp.bfloat16)
    key_part = (jnp.einsum("hqk,qhd->kd", dscore_low, q_part) * score_scale).astype(jnp.bfloat16)
    value_part = jnp.einsum("hqk,qhd->kd", prob_low, g_part).astype(jnp.bfloat16)
    return dq_part.reshape(SEQUENCE_TOKENS, local_heads * HEAD_SIZE), key_part, value_part


def combine_copies(slice_pieces):
    gradient_total = slice_pieces.astype(jnp.float32).reshape(N_DP, KEY_VALUE_HEADS, N_SP // KEY_VALUE_HEADS, SEQUENCE_TOKENS, HEAD_SIZE).sum(axis=2)
    return gradient_total.transpose(0, 2, 1, 3).reshape(ALL_TOKENS, KEY_VALUE_HEADS * HEAD_SIZE).astype(jnp.bfloat16)


def reference(layer_input, queries, keys, values, out_grad, key_value_weight):
    indices = jnp.arange(N_DP * N_SP, dtype=jnp.int32)
    dq_all, key_all, value_all = lax.map(lambda flat_index: group_grads(queries, keys, values, out_grad, flat_index), indices)
    query_grad = dq_all.reshape(N_DP, N_SP, SEQUENCE_TOKENS, (QUERY_HEADS // N_SP) * HEAD_SIZE).transpose(0, 2, 1, 3).reshape(ALL_TOKENS, QUERY_HEADS * HEAD_SIZE)
    key_value_gradient = jnp.concatenate([combine_copies(key_all), combine_copies(value_all)], axis=1)
    input_grad = jnp.dot(key_value_gradient, key_value_weight.T, preferred_element_type=jnp.float32).astype(jnp.bfloat16)
    weight_grad = jnp.dot(layer_input.T, key_value_gradient, preferred_element_type=jnp.float32) * (1.0 / N_DP)
    return query_grad, input_grad, weight_grad
```

```python
import functools
import math

import jax
import jax.numpy as jnp
from jax import lax
from jax.experimental import pallas as pl
from jax.experimental.pallas import tpu as pltpu
from jax.sharding import PartitionSpec as P

HEAD = 128
SCALE = HEAD ** -0.5
SCALE2 = SCALE * math.log2(math.e)
HEADS_AT_ONCE = 4
KEY_ROWS = 1024
f32 = jnp.float32
bf16 = jnp.bfloat16


def dot(a, b, ca, cb):
    return lax.dot_general(a, b, (((ca,), (cb,)), ((), ())), preferred_element_type=f32)


def attend(s, gi, group, q_ref, g_ref, kv_ref, dq_ref, s_scr, dp_scr, dk_scr, dv_scr, kt_scr, dqt_scr):
    tokens = q_ref.shape[0]
    rows = HEADS_AT_ONCE * tokens
    chunks = (s * tokens) // KEY_ROWS + 1
    kcols = pl.ds(gi * HEAD, HEAD)
    vcols = pl.ds((2 + gi) * HEAD, HEAD)

    def keys_of(c):
        return pl.ds(pl.multiple_of(c * KEY_ROWS, KEY_ROWS), KEY_ROWS)

    def prepare(c, _):
        r = keys_of(c)
        kt_scr[:, r] = kv_ref[r, kcols].T
        return 0

    lax.fori_loop(0, chunks, prepare, 0)
    dk_scr[...] = jnp.zeros_like(dk_scr)
    dv_scr[...] = jnp.zeros_like(dv_scr)

    def heads(hb, _):
        first = gi * group + hb * HEADS_AT_ONCE
        cols = [pl.ds(pl.multiple_of((first + i) * HEAD, HEAD), HEAD) for i in range(HEADS_AT_ONCE)]
        q = jnp.concatenate([q_ref[:, h] for h in cols], axis=0)
        g = jnp.concatenate([g_ref[:, h] for h in cols], axis=0)
        qf = q.astype(f32) * SCALE2
        high = qf.astype(bf16)
        low = (qf - high.astype(f32)).astype(bf16)
        q2 = jnp.concatenate([high, low], axis=1)

        def score(c):
            r = keys_of(c)
            k = kv_ref[r, kcols]
            return r, dot(jnp.concatenate([k, k], axis=1), q2, 1, 1)

        def top(x):
            return x.reshape(KEY_ROWS // 8, 8, rows).max(0)

        def add(x):
            return x.reshape(KEY_ROWS // 8, 8, rows).sum(0)

        def first_pass(c, m):
            r, sc = score(c)
            s_scr[r, :] = sc
            return jnp.maximum(m, top(sc))

        m = lax.fori_loop(0, chunks - 1, first_pass, jnp.full((8, rows), -jnp.inf, f32))
        r, sc = score(chunks - 1)
        key = (chunks - 1) * KEY_ROWS + lax.broadcasted_iota(jnp.int32, (KEY_ROWS, rows), 0)
        token = s * tokens + lax.broadcasted_iota(jnp.int32, (KEY_ROWS, rows), 1) % tokens
        sc = jnp.where(key <= token, sc, -jnp.inf)
        s_scr[r, :] = sc
        m = jnp.maximum(m, top(sc)).max(0, keepdims=True)

        def second_pass(c, carry):
            total, rd = carry
            r = keys_of(c)
            e = jnp.exp2(s_scr[r, :] - m)
            s_scr[r, :] = e
            dp = dot(kv_ref[r, vcols], g, 1, 1)
            dp_scr[r, :] = dp
            return total + add(e), rd + add(e * dp)

        zero = jnp.zeros((8, rows), f32)
        total, rd = lax.fori_loop(0, chunks, second_pass, (zero, zero))
        inv = 1.0 / total.sum(0, keepdims=True)
        rd = rd.sum(0, keepdims=True) * inv
        dqt_scr[...] = jnp.zeros_like(dqt_scr)

        def third_pass(c, _):
            r = keys_of(c)
            p = s_scr[r, :] * inv
            ds = (p * (dp_scr[r, :] - rd)).astype(bf16)
            dv_scr[r, :] += dot(p.astype(bf16), g, 1, 0)
            dk_scr[r, :] += dot(ds, q, 1, 0)
            dqt_scr[...] += dot(kt_scr[:, r], ds, 1, 0)
            return 0

        lax.fori_loop(0, chunks, third_pass, 0)
        dq = (dqt_scr[...] * SCALE).T.astype(bf16)
        for i in range(HEADS_AT_ONCE):
            dq_ref[:, cols[i]] = dq[i * tokens : (i + 1) * tokens]
        return 0

    lax.fori_loop(0, group // HEADS_AT_ONCE, heads, 0)


def attention_kernel(q_ref, g_ref, kv_ref, dq_ref, part_ref, s_scr, dp_scr, dk_scr, dv_scr, kt_scr, dqt_scr):
    s = lax.axis_index("sp")
    for gi in range(2):
        attend(s, gi, 16, q_ref, g_ref, kv_ref, dq_ref, s_scr, dp_scr, dk_scr, dv_scr, kt_scr, dqt_scr)
        part_ref[:, gi * HEAD : (gi + 1) * HEAD] = (dk_scr[...] * SCALE).astype(bf16)
        part_ref[:, (2 + gi) * HEAD : (3 + gi) * HEAD] = dv_scr[...].astype(bf16)


def body(layer_input, queries, keys, values, out_grad, key_value_weight):
    n_sp = lax.axis_size("sp")
    n_dp = lax.axis_size("dp")
    tokens, width = queries.shape
    length = tokens * n_sp
    rows = HEADS_AT_ONCE * tokens
    kv = lax.all_gather(jnp.concatenate([keys, values], axis=1), "sp", axis=0, tiled=True)
    vmem = pl.BlockSpec(memory_space=pltpu.VMEM)
    query_grad, part = pl.pallas_call(
        attention_kernel,
        out_shape=[
            jax.ShapeDtypeStruct((tokens, width), bf16),
            jax.ShapeDtypeStruct((length, 4 * HEAD), bf16),
        ],
        in_specs=[vmem] * 3,
        out_specs=[vmem] * 2,
        scratch_shapes=[
            pltpu.VMEM((length, rows), f32),
            pltpu.VMEM((length, rows), f32),
            pltpu.VMEM((length, HEAD), f32),
            pltpu.VMEM((length, HEAD), f32),
            pltpu.VMEM((HEAD, length), bf16),
            pltpu.VMEM((HEAD, rows), f32),
        ],
        compiler_params=pltpu.CompilerParams(vmem_limit_bytes=48 * 2**20),
        cost_estimate=pl.CostEstimate(flops=10 * 2**30, bytes_accessed=8 * 2**20, transcendentals=8 * 2**20),
        name="attention",
    )(queries, out_grad, kv)
    moved = lax.all_to_all(part.reshape(n_sp, tokens, 4 * HEAD), "sp", split_axis=0, concat_axis=0)
    kv_grad = moved.astype(f32).sum(axis=0).astype(bf16)
    spread = layer_input.T.reshape(n_dp, n_sp, width // (n_dp * n_sp), tokens)
    columns = lax.all_to_all(spread, "sp", split_axis=1, concat_axis=1)
    columns = columns.transpose(0, 2, 1, 3).reshape(width // n_sp, length)
    weight = lax.all_gather(key_value_weight, ("dp", "sp"), axis=0, tiled=True)
    kv_grad_all = lax.all_gather(kv_grad, "sp", axis=0, tiled=True)
    input_grad = dot(kv_grad, weight, 1, 1).astype(bf16)
    partial = dot(columns, kv_grad_all, 1, 0).reshape(n_dp, width // (n_dp * n_sp), 4 * HEAD)
    partial = lax.all_to_all(partial, "dp", split_axis=0, concat_axis=0)
    weight_grad = partial.sum(axis=0) * (1.0 / n_dp)
    return query_grad, input_grad, weight_grad


def solution(mesh):
    placed = P(("dp", "sp"), None)
    return jax.shard_map(
        body,
        mesh=mesh,
        in_specs=(placed,) * 6,
        out_specs=(placed,) * 3,
        check_vma=False,
    )
```

```python
import functools
import math

import jax
import jax.numpy as jnp
from jax import lax
from jax.experimental import pallas as pl
from jax.experimental.pallas import tpu as pltpu
from jax.sharding import PartitionSpec as P

HEAD = 128
SCALE = HEAD ** -0.5
SCALE2 = SCALE * math.log2(math.e)
HEADS_AT_ONCE = 4
KEY_ROWS = 1024
f32 = jnp.float32
bf16 = jnp.bfloat16


def dot(a, b, ca, cb):
    return lax.dot_general(a, b, (((ca,), (cb,)), ((), ())), preferred_element_type=f32)


def attend_heads(s, first, key_rows, q_ref, g_ref, kv_ref, dq_ref, s_scr, dp_scr, dk_scr, dv_scr, kt_scr, dqt_scr):
    tokens = q_ref.shape[0]
    rows = HEADS_AT_ONCE * tokens
    chunks = (s * tokens) // key_rows + 1

    def keys_of(c):
        return pl.ds(pl.multiple_of(c * key_rows, key_rows), key_rows)

    cols = [pl.ds(pl.multiple_of((first + i) * HEAD, HEAD), HEAD) for i in range(HEADS_AT_ONCE)]
    q = jnp.concatenate([q_ref[:, h] for h in cols], axis=0)
    g = jnp.concatenate([g_ref[:, h] for h in cols], axis=0)
    qf = q.astype(f32) * SCALE2
    high = qf.astype(bf16)
    low = (qf - high.astype(f32)).astype(bf16)
    q2 = jnp.concatenate([high, low], axis=1)

    def score(c):
        r = keys_of(c)
        k = kv_ref[r, :HEAD]
        return r, dot(jnp.concatenate([k, k], axis=1), q2, 1, 1)

    def top(x):
        return x.reshape(key_rows // 8, 8, rows).max(0)

    def add(x):
        return x.reshape(key_rows // 8, 8, rows).sum(0)

    def first_pass(c, m):
        r, sc = score(c)
        s_scr[r, :] = sc
        return jnp.maximum(m, top(sc))

    m = lax.fori_loop(0, chunks - 1, first_pass, jnp.full((8, rows), -jnp.inf, f32))
    r, sc = score(chunks - 1)
    key = (chunks - 1) * key_rows + lax.broadcasted_iota(jnp.int32, (key_rows, rows), 0)
    token = s * tokens + lax.broadcasted_iota(jnp.int32, (key_rows, rows), 1) % tokens
    sc = jnp.where(key <= token, sc, -jnp.inf)
    s_scr[r, :] = sc
    m = jnp.maximum(m, top(sc)).max(0, keepdims=True)

    def second_pass(c, carry):
        total, rd = carry
        r = keys_of(c)
        e = jnp.exp2(s_scr[r, :] - m)
        s_scr[r, :] = e
        dp = dot(kv_ref[r, HEAD:], g, 1, 1)
        dp_scr[r, :] = dp
        return total + add(e), rd + add(e * dp)

    zero = jnp.zeros((8, rows), f32)
    total, rd = lax.fori_loop(0, chunks, second_pass, (zero, zero))
    inv = 1.0 / total.sum(0, keepdims=True)
    rd = rd.sum(0, keepdims=True) * inv
    dqt_scr[...] = jnp.zeros_like(dqt_scr)

    def third_pass(c, _):
        r = keys_of(c)
        p = s_scr[r, :] * inv
        ds = (p * (dp_scr[r, :] - rd)).astype(bf16)
        dv_scr[r, :] += dot(p.astype(bf16), g, 1, 0)
        dk_scr[r, :] += dot(ds, q, 1, 0)
        dqt_scr[...] += dot(kt_scr[:, r], ds, 1, 0)
        return 0

    lax.fori_loop(0, chunks, third_pass, 0)
    dq = (dqt_scr[...] * SCALE).T.astype(bf16)
    for i in range(HEADS_AT_ONCE):
        dq_ref[:, cols[i]] = dq[i * tokens : (i + 1) * tokens]


def kernel(
    n_dp, n_sp,
    x_ref, q_ref, k_ref, v_ref, g_ref, w_ref,
    dq_ref, ig_ref, wg_ref,
    s_scr, dp_scr, dk_scr, dv_scr, kt_scr, dqt_scr,
    kv_all, xt, x_all, w_all, part, part_in, grad_all, sum_scr, row_out, row_in,
    kv_send, kv_recv, x_send, x_recv, w_send, w_recv, right_send, left_send, ring_recv, pair_send, pair_recv,
    part_send, part_recv, grad_send, grad_recv, row_send, row_recv,
):
    d = lax.axis_index("dp")
    s = lax.axis_index("sp")
    n_z = n_dp // 2
    z, core = d // 2, d % 2
    tokens = q_ref.shape[0]
    length = tokens * n_sp
    key_rows = min(KEY_ROWS, length)
    group = q_ref.shape[1] // HEAD // 2
    per_group = group // HEADS_AT_ONCE
    w_rows = w_ref.shape[0]
    block = n_sp * w_rows

    barrier = pltpu.get_barrier_semaphore()

    def greet(n, me, axis):
        def one(i, _):
            pl.semaphore_signal(
                barrier, inc=1, device_id={axis: lax.rem(me + i, n)}, device_id_type=pl.DeviceIdType.MESH
            )
            return 0

        lax.fori_loop(1, n, one, 0)

    greet(n_sp, s, "sp")
    greet(n_dp, d, "dp")

    def copy(src, dst, send, recv, axis, to):
        return pltpu.make_async_remote_copy(
            src_ref=src, dst_ref=dst, send_sem=send, recv_sem=recv,
            device_id={axis: to}, device_id_type=pl.DeviceIdType.MESH,
        )

    def each_sp(f):
        def one(i, _):
            f(lax.rem(s + i, n_sp))
            return 0

        lax.fori_loop(1, n_sp, one, 0)

    def each_dp(f):
        def one(i, _):
            f(lax.rem(d + i, n_dp))
            return 0

        lax.fori_loop(1, n_dp, one, 0)

    def span(i, size):
        return pl.ds(pl.multiple_of(i * size, size), size)

    own = span(s, tokens)

    def kv_copy(gi, t, owner):
        r = span(owner, tokens)
        return copy(kv_all.at[gi, r], kv_all.at[gi, r], kv_send.at[gi, t], kv_recv.at[gi, owner], "sp", t)

    def w_copy(t, owner):
        r = pl.ds(pl.multiple_of(d * block + owner * w_rows, w_rows), w_rows)
        return copy(w_all.at[r], w_all.at[r], w_send.at[t], w_recv.at[owner], "sp", t)

    def ring_copy(zb, to, send):
        r = span(zb * 2 + core, block)
        return copy(w_all.at[r], w_all.at[r], send, ring_recv.at[zb], "dp", to * 2 + core)

    def pair_copy(zb, c):
        r = span(zb * 2 + c, block)
        return copy(w_all.at[r], w_all.at[r], pair_send.at[zb], pair_recv.at[zb], "dp", z * 2 + 1 - core)

    def x_copy(t, owner):
        return copy(xt.at[t], x_all.at[owner], x_send.at[t], x_recv.at[owner], "sp", t)

    def part_copy(gi, t, owner):
        return copy(part.at[gi, t], part_in.at[gi, owner], part_send.at[gi, t], part_recv.at[gi, owner], "sp", t)

    def grad_copy(gi, t, owner):
        return copy(
            grad_all.at[gi, owner], grad_all.at[gi, owner], grad_send.at[gi, t], grad_recv.at[gi, owner], "sp", t
        )

    def row_copy(gi, t, owner):
        return copy(
            row_out.at[gi, span(t, w_rows)], row_in.at[gi, owner], row_send.at[gi, t], row_recv.at[gi, owner], "dp", t
        )

    for gi in range(2):
        kv_all[gi, own, :HEAD] = k_ref[:, gi * HEAD : (gi + 1) * HEAD]
        kv_all[gi, own, HEAD:] = v_ref[:, gi * HEAD : (gi + 1) * HEAD]

        def clear(t, _):
            kv_all[gi, span(t, tokens)] = jnp.zeros((tokens, 2 * HEAD), bf16)
            return 0

        lax.fori_loop(s + 1, n_sp, clear, 0)
    w_all[pl.ds(pl.multiple_of(d * block + s * w_rows, w_rows), w_rows)] = w_ref[...]
    pl.semaphore_wait(barrier, n_sp + n_dp - 2)

    for gi in range(2):

        def send_kv(t, _):
            kv_copy(gi, t, s).start()
            return 0

        lax.fori_loop(s + 1, n_sp, send_kv, 0)
    each_sp(lambda t: w_copy(t, s).start())

    def transpose(j, _):
        columns = x_ref[:, span(j, block)].T
        xt[:, span(j, w_rows)] = columns.reshape(n_sp, w_rows, tokens)
        return 0

    lax.fori_loop(0, n_dp, transpose, 0)
    x_all[s] = xt[s]
    each_sp(lambda t: x_copy(t, s).start())

    right = lax.rem(z + 1, n_z)
    left = lax.rem(z + n_z - 1, n_z)
    n_right = n_z // 2
    n_left = n_z - 1 - n_right

    def ring_step(k):
        @pl.when(k == 0)
        def _():
            each_sp(lambda t: w_copy(s, t).wait_recv())
            ring_copy(z, right, right_send.at[0]).start()
            if n_left:
                ring_copy(z, left, left_send.at[0]).start()
            pair_copy(z, core).start()

        @pl.when((k >= 1) & (k <= n_right))
        def _():
            zb = lax.rem(z + n_z - k, n_z)
            ring_copy(zb, right, right_send.at[0]).wait_recv()

            @pl.when(k < n_right)
            def _():
                ring_copy(zb, right, right_send.at[k]).start()

            pair_copy(zb, core).start()

        @pl.when((k >= 1) & (k <= n_left))
        def _():
            zb = lax.rem(z + k, n_z)
            ring_copy(zb, left, left_send.at[0]).wait_recv()

            @pl.when(k < n_left)
            def _():
                ring_copy(zb, left, left_send.at[k]).start()

            pair_copy(zb, core).start()

    def reduce(gi):
        def one(t, _):
            part_copy(gi, s, t).wait_recv()
            sum_scr[:tokens] += part_in[gi, t].astype(f32)
            return 0

        sum_scr[:tokens] = part[gi, s].astype(f32)
        lax.fori_loop(s + 1, n_sp, one, 0)
        grad_all[gi, s] = sum_scr[:tokens].astype(bf16)
        each_sp(lambda t: grad_copy(gi, t, s).start())

    steps = 2 * per_group
    for gi in range(2):

        def wait_kv(t, _):
            kv_copy(gi, s, t).wait_recv()
            return 0

        lax.fori_loop(0, s, wait_kv, 0)

        def prepare(c, _):
            r = span(c, key_rows)
            kt_scr[:, r] = kv_all[gi, r, :HEAD].T
            dk_scr[r] = jnp.zeros((key_rows, HEAD), f32)
            dv_scr[r] = jnp.zeros((key_rows, HEAD), f32)
            return 0

        lax.fori_loop(0, length // key_rows, prepare, 0)

        def heads(hb, _):
            it = gi * per_group + hb

            @pl.when(it >= 1)
            def _():
                ring_step(it - 1)

            if gi == 1:

                @pl.when(it == steps * 3 // 4)
                def _():
                    reduce(0)

            attend_heads(
                s, gi * group + hb * HEADS_AT_ONCE, key_rows,
                q_ref, g_ref, kv_all.at[gi], dq_ref, s_scr, dp_scr, dk_scr, dv_scr, kt_scr, dqt_scr,
            )
            return 0

        lax.fori_loop(0, per_group, heads, 0)

        def give(t, _):
            r = span(t, tokens)
            part[gi, t, :, :HEAD] = (dk_scr[r] * SCALE).astype(bf16)
            part[gi, t, :, HEAD:] = dv_scr[r].astype(bf16)

            @pl.when(t < s)
            def _():
                part_copy(gi, t, s).start()

            return 0

        lax.fori_loop(0, s + 1, give, 0)

    for k in range(steps - 1, n_right + 1):
        ring_step(k)

    def weight_rows(gi):
        each_sp(lambda t: grad_copy(gi, s, t).wait_recv())
        sum_scr[...] = jnp.zeros_like(sum_scr)

        def one(i, _):
            a = jnp.concatenate([x_all[2 * i], x_all[2 * i + 1]], axis=1)
            b = jnp.concatenate([grad_all[gi, 2 * i], grad_all[gi, 2 * i + 1]], axis=0)
            sum_scr[...] += dot(a, b, 1, 0)
            return 0

        lax.fori_loop(0, n_sp // 2, one, 0)
        row_out[gi] = sum_scr[: n_dp * w_rows].astype(bf16)
        each_dp(lambda t: row_copy(gi, t, d).start())

    each_sp(lambda t: x_copy(s, t).wait_recv())
    weight_rows(0)
    reduce(1)

    def wait_pair(zb, _):
        pair_copy(zb, 1 - core).wait_recv()
        return 0

    lax.fori_loop(0, n_z, wait_pair, 0)
    mine = jnp.concatenate(
        [grad_all[0, s, :, :HEAD], grad_all[1, s, :, :HEAD], grad_all[0, s, :, HEAD:], grad_all[1, s, :, HEAD:]], axis=1
    )

    def inputs(j, _):
        r = span(j, block)
        ig_ref[:, r] = dot(mine, w_all[r], 1, 1).astype(bf16)
        return 0

    lax.fori_loop(0, n_dp, inputs, 0)
    weight_rows(1)

    for gi in range(2):

        def one(i, total):
            t = lax.rem(d + i, n_dp)
            row_copy(gi, d, t).wait_recv()
            return total + row_in[gi, t].astype(f32)

        total = lax.fori_loop(1, n_dp, one, row_out[gi, span(d, w_rows)].astype(f32)) * (1.0 / n_dp)
        wg_ref[:, gi * HEAD : (gi + 1) * HEAD] = total[:, :HEAD]
        wg_ref[:, (2 + gi) * HEAD : (3 + gi) * HEAD] = total[:, HEAD:]

    for gi in range(2):

        def sent_kv(t, _):
            kv_copy(gi, t, s).wait_send()
            return 0

        def sent_part(t, _):
            part_copy(gi, t, s).wait_send()
            return 0

        lax.fori_loop(s + 1, n_sp, sent_kv, 0)
        lax.fori_loop(0, s, sent_part, 0)
        each_sp(lambda t: grad_copy(gi, t, s).wait_send())
        each_dp(lambda t: row_copy(gi, t, d).wait_send())
    each_sp(lambda t: w_copy(t, s).wait_send())
    each_sp(lambda t: x_copy(t, s).wait_send())

    def sent_pair(zb, _):
        pair_copy(zb, core).wait_send()
        return 0

    lax.fori_loop(0, n_z, sent_pair, 0)
    for k in range(n_right):
        ring_copy(z, right, right_send.at[k]).wait_send()
    for k in range(n_left):
        ring_copy(z, left, left_send.at[k]).wait_send()


def body(layer_input, queries, keys, values, out_grad, key_value_weight):
    n_sp = lax.axis_size("sp")
    n_dp = lax.axis_size("dp")
    tokens, q_width = queries.shape
    width = layer_input.shape[1]
    w_rows, kv_width = key_value_weight.shape
    length = tokens * n_sp
    rows = HEADS_AT_ONCE * tokens
    sp_rows = width // n_sp
    sem = pltpu.SemaphoreType.DMA
    vmem = pl.BlockSpec(memory_space=pltpu.VMEM)
    return pl.pallas_call(
        functools.partial(kernel, n_dp, n_sp),
        out_shape=(
            jax.ShapeDtypeStruct((tokens, q_width), bf16),
            jax.ShapeDtypeStruct((tokens, width), bf16),
            jax.ShapeDtypeStruct((w_rows, kv_width), f32),
        ),
        in_specs=[vmem] * 6,
        out_specs=(vmem,) * 3,
        scratch_shapes=[
            pltpu.VMEM((length, rows), f32),
            pltpu.VMEM((length, rows), f32),
            pltpu.VMEM((length, HEAD), f32),
            pltpu.VMEM((length, HEAD), f32),
            pltpu.VMEM((HEAD, length), bf16),
            pltpu.VMEM((HEAD, rows), f32),
            pltpu.VMEM((2, length, 2 * HEAD), bf16),
            pltpu.VMEM((n_sp, sp_rows, tokens), bf16),
            pltpu.VMEM((n_sp, sp_rows, tokens), bf16),
            pltpu.VMEM((width, kv_width), bf16),
            pltpu.VMEM((2, n_sp, tokens, 2 * HEAD), bf16),
            pltpu.VMEM((2, n_sp, tokens, 2 * HEAD), bf16),
            pltpu.VMEM((2, n_sp, tokens, 2 * HEAD), bf16),
            pltpu.VMEM((max(sp_rows, tokens), 2 * HEAD), f32),
            pltpu.VMEM((2, sp_rows, 2 * HEAD), bf16),
            pltpu.VMEM((2, n_dp, w_rows, 2 * HEAD), bf16),
            sem((2, n_sp)), sem((2, n_sp)),
            sem((n_sp,)), sem((n_sp,)),
            sem((n_sp,)), sem((n_sp,)),
            sem((n_dp,)), sem((n_dp,)), sem((n_dp,)), sem((n_dp,)), sem((n_dp,)),
            sem((2, n_sp)), sem((2, n_sp)),
            sem((2, n_sp)), sem((2, n_sp)),
            sem((2, n_dp)), sem((2, n_dp)),
        ],
        compiler_params=pltpu.CompilerParams(
            collective_id=0, has_side_effects=True, vmem_limit_bytes=56 * 2**20
        ),
        cost_estimate=pl.CostEstimate(flops=12 * 2**30, bytes_accessed=8 * 2**20, transcendentals=8 * 2**20),
        name="attention_grads",
    )(layer_input, queries, keys, values, out_grad, key_value_weight)


def solution(mesh):
    placed = P(("dp", "sp"), None)
    return jax.shard_map(
        body,
        mesh=mesh,
        in_specs=(placed,) * 6,
        out_specs=(placed,) * 3,
        check_vma=False,
    )
```

```python
import functools
import math

import jax
import jax.numpy as jnp
from jax import lax
from jax.experimental import pallas as pl
from jax.experimental.pallas import tpu as pltpu
from jax.sharding import PartitionSpec as P

HEAD = 128
SCALE = HEAD ** -0.5
SCALE2 = SCALE * math.log2(math.e)
HEADS_AT_ONCE = 4
KEY_ROWS = 1024
f32 = jnp.float32
bf16 = jnp.bfloat16


def dot(a, b, ca, cb):
    return lax.dot_general(a, b, (((ca,), (cb,)), ((), ())), preferred_element_type=f32)


def attend_heads(s, first, key_rows, q_ref, g_ref, kv_ref, dq_ref, s_scr, dp_scr, dk_scr, dv_scr, kt_scr, dqt_scr):
    tokens = q_ref.shape[0]
    rows = HEADS_AT_ONCE * tokens
    chunks = (s * tokens) // key_rows + 1

    def keys_of(c):
        return pl.ds(pl.multiple_of(c * key_rows, key_rows), key_rows)

    cols = [pl.ds(pl.multiple_of((first + i) * HEAD, HEAD), HEAD) for i in range(HEADS_AT_ONCE)]
    q = jnp.concatenate([q_ref[:, h] for h in cols], axis=0)
    g = jnp.concatenate([g_ref[:, h] for h in cols], axis=0)
    qf = q.astype(f32) * SCALE2
    high = qf.astype(bf16)
    low = (qf - high.astype(f32)).astype(bf16)
    q2 = jnp.concatenate([high, low], axis=1)

    def score(c):
        r = keys_of(c)
        k = kv_ref[r, :HEAD]
        return r, dot(jnp.concatenate([k, k], axis=1), q2, 1, 1)

    def top(x):
        return x.reshape(key_rows // 8, 8, rows).max(0)

    def add(x):
        return x.reshape(key_rows // 8, 8, rows).sum(0)

    def first_pass(c, m):
        r, sc = score(c)
        s_scr[r, :] = sc
        return jnp.maximum(m, top(sc))

    m = lax.fori_loop(0, chunks - 1, first_pass, jnp.full((8, rows), -jnp.inf, f32))
    r, sc = score(chunks - 1)
    key = (chunks - 1) * key_rows + lax.broadcasted_iota(jnp.int32, (key_rows, rows), 0)
    token = s * tokens + lax.broadcasted_iota(jnp.int32, (key_rows, rows), 1) % tokens
    sc = jnp.where(key <= token, sc, -jnp.inf)
    s_scr[r, :] = sc
    m = jnp.maximum(m, top(sc)).max(0, keepdims=True)

    def second_pass(c, carry):
        total, rd = carry
        r = keys_of(c)
        e = jnp.exp2(s_scr[r, :] - m)
        s_scr[r, :] = e
        dp = dot(kv_ref[r, HEAD:], g, 1, 1)
        dp_scr[r, :] = dp
        return total + add(e), rd + add(e * dp)

    zero = jnp.zeros((8, rows), f32)
    total, rd = lax.fori_loop(0, chunks, second_pass, (zero, zero))
    inv = 1.0 / total.sum(0, keepdims=True)
    rd = rd.sum(0, keepdims=True) * inv
    dqt_scr[...] = jnp.zeros_like(dqt_scr)

    def third_pass(c, _):
        r = keys_of(c)
        p = s_scr[r, :] * inv
        ds = (p * (dp_scr[r, :] - rd)).astype(bf16)
        dv_scr[r, :] += dot(p.astype(bf16), g, 1, 0)
        dk_scr[r, :] += dot(ds, q, 1, 0)
        dqt_scr[...] += dot(kt_scr[:, r], ds, 1, 0)
        return 0

    lax.fori_loop(0, chunks, third_pass, 0)
    dq = (dqt_scr[...] * SCALE).T.astype(bf16)
    for i in range(HEADS_AT_ONCE):
        dq_ref[:, cols[i]] = dq[i * tokens : (i + 1) * tokens]


def kernel(
    n_dp, n_sp, n_y,
    x_ref, q_ref, k_ref, v_ref, g_ref, w_ref,
    dq_ref, ig_ref, wg_ref,
    s_scr, dp_scr, dk_scr, dv_scr, kt_scr, dqt_scr,
    kv_all, xt, x_all, w_all, part, part_in, grad_all, sum_scr, row_out, row_in,
    kv_send, kv_recv, x_send, x_recv, w_send, w_recv, right_send, left_send, ring_recv, pair_send, pair_recv,
    part_send, part_recv, near_send, near_recv, far_send, far_recv, relay_send, relay_recv, row_send, row_recv,
):
    d = lax.axis_index("dp")
    s = lax.axis_index("sp")
    n_z = n_dp // 2
    n_x = n_sp // n_y
    sx, sy = s // n_y, s % n_y
    z, core = d // 2, d % 2
    tokens = q_ref.shape[0]
    length = tokens * n_sp
    key_rows = min(KEY_ROWS, length)
    group = q_ref.shape[1] // HEAD // 2
    per_group = group // HEADS_AT_ONCE
    w_rows = w_ref.shape[0]
    block = n_sp * w_rows

    barrier = pltpu.get_barrier_semaphore()

    def greet(n, me, axis):
        def one(i, _):
            pl.semaphore_signal(
                barrier, inc=1, device_id={axis: lax.rem(me + i, n)}, device_id_type=pl.DeviceIdType.MESH
            )
            return 0

        lax.fori_loop(1, n, one, 0)

    greet(n_sp, s, "sp")
    greet(n_dp, d, "dp")

    def copy(src, dst, send, recv, axis, to):
        return pltpu.make_async_remote_copy(
            src_ref=src, dst_ref=dst, send_sem=send, recv_sem=recv,
            device_id={axis: to}, device_id_type=pl.DeviceIdType.MESH,
        )

    def each_sp(f):
        def one(i, _):
            f(lax.rem(s + i, n_sp))
            return 0

        lax.fori_loop(1, n_sp, one, 0)

    def each_dp(f):
        def one(i, _):
            f(lax.rem(d + i, n_dp))
            return 0

        lax.fori_loop(1, n_dp, one, 0)

    def span(i, size):
        return pl.ds(pl.multiple_of(i * size, size), size)

    own = span(s, tokens)

    def kv_copy(gi, t, owner):
        r = span(owner, tokens)
        return copy(kv_all.at[gi, r], kv_all.at[gi, r], kv_send.at[gi, t], kv_recv.at[gi, owner], "sp", t)

    def w_copy(t, owner):
        r = pl.ds(pl.multiple_of(d * block + owner * w_rows, w_rows), w_rows)
        return copy(w_all.at[r], w_all.at[r], w_send.at[t], w_recv.at[owner], "sp", t)

    def ring_copy(zb, to, send):
        r = span(zb * 2 + core, block)
        return copy(w_all.at[r], w_all.at[r], send, ring_recv.at[zb], "dp", to * 2 + core)

    def pair_copy(zb, c):
        r = span(zb * 2 + c, block)
        return copy(w_all.at[r], w_all.at[r], pair_send.at[zb], pair_recv.at[zb], "dp", z * 2 + 1 - core)

    def x_copy(t, owner):
        return copy(xt.at[t], x_all.at[owner], x_send.at[t], x_recv.at[owner], "sp", t)

    def part_copy(gi, t, owner):
        return copy(part.at[gi, t], part_in.at[gi, owner], part_send.at[gi, t], part_recv.at[gi, owner], "sp", t)

    half_rows = tokens // 2
    ring = (n_x, n_y)
    at_ring = (sx, sy)

    def place(h, far, near):
        r = slice(h * half_rows, (h + 1) * half_rows)
        return (far, near, r) if h == 0 else (near, far, r)

    def partner(h, i, last):
        return i * n_y + sy if (h == 0) == last else sx * n_y + i

    def near_copy(gi, h, i, owner):
        ref = grad_all.at[(gi,) + place(h, at_ring[h], owner)]
        return copy(ref, ref, near_send.at[gi, h, i], near_recv.at[gi, h, owner], "sp", partner(h, i, False))

    def far_copy(gi, h, side, owner):
        ref = grad_all.at[(gi,) + place(h, owner, slice(None))]
        to = lax.rem(at_ring[h] + (1, ring[h] - 1)[side], ring[h])
        return copy(ref, ref, far_send.at[gi, h, side], far_recv.at[gi, h, side], "sp", partner(h, to, True))

    def relay_copy(gi, h, side, owner):
        middle = ring[1 - h] // 2
        which = slice(0, middle) if side == 0 else slice(middle, ring[1 - h])
        ref = grad_all.at[(gi,) + place(h, owner, which)]
        to = lax.rem(at_ring[h] + (1, ring[h] - 1)[side], ring[h])
        return copy(ref, ref, relay_send.at[gi, h, side], relay_recv.at[gi, h, side], "sp", partner(h, to, True))

    def others(h, f):
        def one(i, _):
            f(lax.rem(at_ring[1 - h] + i, ring[1 - h]))
            return 0

        lax.fori_loop(1, ring[1 - h], one, 0)

    def sides(h):
        return min(ring[h] - 1, 2)

    def behind(h, side, n):
        return lax.rem(at_ring[h] + ring[h] + (-n, n)[side], ring[h])

    def gather_near(gi):
        for h in range(2):
            others(h, lambda i: near_copy(gi, h, i, at_ring[1 - h]).start())

    def gather_far(gi):
        for h in range(2):
            others(h, lambda i: near_copy(gi, h, at_ring[1 - h], i).wait_recv())
            for side in range(sides(h)):
                far_copy(gi, h, side, at_ring[h]).start()

    def gather_relay(gi):
        for h in range(2):
            for side in range(sides(h)):
                far_copy(gi, h, side, behind(h, side, 1)).wait_recv()
                if ring[h] == 4:
                    relay_copy(gi, h, side, behind(h, side, 1)).start()

    def gather_end(gi):
        for h in range(2):
            if ring[h] == 4:
                for side in range(2):
                    relay_copy(gi, h, side, behind(h, side, 2)).wait_recv()

    def gather_sent(gi):
        for h in range(2):
            others(h, lambda i: near_copy(gi, h, i, at_ring[1 - h]).wait_send())
            for side in range(sides(h)):
                far_copy(gi, h, side, at_ring[h]).wait_send()
                if ring[h] == 4:
                    relay_copy(gi, h, side, behind(h, side, 1)).wait_send()

    def row_copy(gi, t, owner):
        return copy(
            row_out.at[gi, span(t, w_rows)], row_in.at[gi, owner], row_send.at[gi, t], row_recv.at[gi, owner], "dp", t
        )

    for gi in range(2):
        kv_all[gi, own, :HEAD] = k_ref[:, gi * HEAD : (gi + 1) * HEAD]
        kv_all[gi, own, HEAD:] = v_ref[:, gi * HEAD : (gi + 1) * HEAD]

        def clear(t, _):
            kv_all[gi, span(t, tokens)] = jnp.zeros((tokens, 2 * HEAD), bf16)
            return 0

        lax.fori_loop(s + 1, n_sp, clear, 0)
    w_all[pl.ds(pl.multiple_of(d * block + s * w_rows, w_rows), w_rows)] = w_ref[...]
    def transpose(j, _):
        columns = x_ref[:, span(j, block)].T
        xt[:, span(j, w_rows)] = columns.reshape(n_sp, w_rows, tokens)
        return 0

    lax.fori_loop(0, n_dp, transpose, 0)
    x_all[s] = xt[s]
    pl.semaphore_wait(barrier, n_sp + n_dp - 2)

    def send_kv(gi):
        def one(t, _):
            kv_copy(gi, t, s).start()
            return 0

        lax.fori_loop(s + 1, n_sp, one, 0)

    def sent_kv(gi):
        def one(t, _):
            kv_copy(gi, t, s).wait_send()
            return 0

        lax.fori_loop(s + 1, n_sp, one, 0)

    send_kv(0)


    right = lax.rem(z + 1, n_z)
    left = lax.rem(z + n_z - 1, n_z)
    n_right = n_z // 2
    n_left = n_z - 1 - n_right

    def ring_step(k):
        @pl.when(k == 0)
        def _():
            each_sp(lambda t: w_copy(s, t).wait_recv())
            if n_right:
                ring_copy(z, right, right_send.at[0]).start()
            if n_left:
                ring_copy(z, left, left_send.at[0]).start()
            pair_copy(z, core).start()

        @pl.when((k >= 1) & (k <= n_right))
        def _():
            zb = lax.rem(z + n_z - k, n_z)
            ring_copy(zb, right, right_send.at[0]).wait_recv()

            @pl.when(k < n_right)
            def _():
                ring_copy(zb, right, right_send.at[k]).start()

            pair_copy(zb, core).start()

        @pl.when((k >= 1) & (k <= n_left))
        def _():
            zb = lax.rem(z + k, n_z)
            ring_copy(zb, left, left_send.at[0]).wait_recv()

            @pl.when(k < n_left)
            def _():
                ring_copy(zb, left, left_send.at[k]).start()

            pair_copy(zb, core).start()

    def reduce(gi):
        def one(t, _):
            part_copy(gi, s, t).wait_recv()
            sum_scr[:tokens] += part_in[gi, t].astype(f32)
            return 0

        sum_scr[:tokens] = part[gi, s].astype(f32)
        lax.fori_loop(s + 1, n_sp, one, 0)
        grad_all[gi, sx, sy] = sum_scr[:tokens].astype(bf16)
        gather_near(gi)

    steps = 2 * per_group
    for gi in range(2):

        def wait_kv(t, _):
            kv_copy(gi, s, t).wait_recv()
            return 0

        lax.fori_loop(0, s, wait_kv, 0)

        def prepare(c, _):
            r = span(c, key_rows)
            kt_scr[:, r] = kv_all[gi, r, :HEAD].T
            dk_scr[r] = jnp.zeros((key_rows, HEAD), f32)
            dv_scr[r] = jnp.zeros((key_rows, HEAD), f32)
            return 0

        lax.fori_loop(0, length // key_rows, prepare, 0)

        def heads(hb, _):
            it = gi * per_group + hb

            if gi == 0:

                @pl.when(hb == 0)
                def _():
                    sent_kv(0)
                    send_kv(1)
                    each_sp(lambda t: w_copy(t, s).start())

            @pl.when(it == 1)
            def _():
                each_sp(lambda t: x_copy(t, s).start())

            @pl.when(it % 2 == 1)
            def _():
                ring_step(it // 2)

            if gi == 1:

                @pl.when(it == steps - 2)
                def _():
                    reduce(0)

                @pl.when(it == steps - 1)
                def _():
                    gather_far(0)

            attend_heads(
                s, gi * group + hb * HEADS_AT_ONCE, key_rows,
                q_ref, g_ref, kv_all.at[gi], dq_ref, s_scr, dp_scr, dk_scr, dv_scr, kt_scr, dqt_scr,
            )
            return 0

        lax.fori_loop(0, per_group, heads, 0)

        def give(t, _):
            r = span(t, tokens)
            part[gi, t, :, :HEAD] = (dk_scr[r] * SCALE).astype(bf16)
            part[gi, t, :, HEAD:] = dv_scr[r].astype(bf16)

            @pl.when(t < s)
            def _():
                part_copy(gi, t, s).start()

            return 0

        lax.fori_loop(0, s + 1, give, 0)

    for k in range(steps // 2, n_right + 1):
        ring_step(k)
    gather_relay(0)

    def weight_rows(gi):
        gather_end(gi)
        sum_scr[...] = jnp.zeros_like(sum_scr)

        def one(i, _):
            a = jnp.concatenate([x_all[2 * i], x_all[2 * i + 1]], axis=1)
            j = 2 * i
            b = jnp.concatenate([grad_all[gi, j // n_y, j % n_y], grad_all[gi, j // n_y, j % n_y + 1]], axis=0)
            sum_scr[...] += dot(a, b, 1, 0)
            return 0

        lax.fori_loop(0, n_sp // 2, one, 0)
        row_out[gi] = sum_scr[: n_dp * w_rows].astype(bf16)
        each_dp(lambda t: row_copy(gi, t, d).start())

    each_sp(lambda t: x_copy(s, t).wait_recv())
    weight_rows(0)
    reduce(1)

    def wait_pair(zb, _):
        pair_copy(zb, 1 - core).wait_recv()
        return 0

    lax.fori_loop(0, n_z, wait_pair, 0)
    mine = jnp.concatenate(
        [grad_all[gi, sx, sy, :, c] for c in (slice(0, HEAD), slice(HEAD, 2 * HEAD)) for gi in range(2)], axis=1
    )

    def inputs(j, _):
        r = span(j, block)
        ig_ref[:, r] = dot(mine, w_all[r], 1, 1).astype(bf16)
        return 0

    lax.fori_loop(0, n_dp // 2, inputs, 0)
    gather_far(1)
    lax.fori_loop(n_dp // 2, n_dp, inputs, 0)
    gather_relay(1)
    weight_rows(1)

    for gi in range(2):

        def one(i, total):
            t = lax.rem(d + i, n_dp)
            row_copy(gi, d, t).wait_recv()
            return total + row_in[gi, t].astype(f32)

        total = lax.fori_loop(1, n_dp, one, row_out[gi, span(d, w_rows)].astype(f32)) * (1.0 / n_dp)
        wg_ref[:, gi * HEAD : (gi + 1) * HEAD] = total[:, :HEAD]
        wg_ref[:, (2 + gi) * HEAD : (3 + gi) * HEAD] = total[:, HEAD:]

    for gi in range(2):

        def sent_part(t, _):
            part_copy(gi, t, s).wait_send()
            return 0

        lax.fori_loop(0, s, sent_part, 0)
        gather_sent(gi)
        each_dp(lambda t: row_copy(gi, t, d).wait_send())
    sent_kv(1)
    each_sp(lambda t: w_copy(t, s).wait_send())
    each_sp(lambda t: x_copy(t, s).wait_send())

    def sent_pair(zb, _):
        pair_copy(zb, core).wait_send()
        return 0

    lax.fori_loop(0, n_z, sent_pair, 0)
    for k in range(n_right):
        ring_copy(z, right, right_send.at[k]).wait_send()
    for k in range(n_left):
        ring_copy(z, left, left_send.at[k]).wait_send()


def body(layer_input, queries, keys, values, out_grad, key_value_weight):
    n_sp = lax.axis_size("sp")
    n_dp = lax.axis_size("dp")
    n_y = 4 if n_sp % 4 == 0 and n_sp > 8 else 2
    tokens, q_width = queries.shape
    width = layer_input.shape[1]
    w_rows, kv_width = key_value_weight.shape
    length = tokens * n_sp
    rows = HEADS_AT_ONCE * tokens
    sp_rows = width // n_sp
    sem = pltpu.SemaphoreType.DMA
    vmem = pl.BlockSpec(memory_space=pltpu.VMEM)
    return pl.pallas_call(
        functools.partial(kernel, n_dp, n_sp, n_y),
        out_shape=(
            jax.ShapeDtypeStruct((tokens, q_width), bf16),
            jax.ShapeDtypeStruct((tokens, width), bf16),
            jax.ShapeDtypeStruct((w_rows, kv_width), f32),
        ),
        in_specs=[vmem] * 6,
        out_specs=(vmem,) * 3,
        scratch_shapes=[
            pltpu.VMEM((length, rows), f32),
            pltpu.VMEM((length, rows), f32),
            pltpu.VMEM((length, HEAD), f32),
            pltpu.VMEM((length, HEAD), f32),
            pltpu.VMEM((HEAD, length), bf16),
            pltpu.VMEM((HEAD, rows), f32),
            pltpu.VMEM((2, length, 2 * HEAD), bf16),
            pltpu.VMEM((n_sp, sp_rows, tokens), bf16),
            pltpu.VMEM((n_sp, sp_rows, tokens), bf16),
            pltpu.VMEM((width, kv_width), bf16),
            pltpu.VMEM((2, n_sp, tokens, 2 * HEAD), bf16),
            pltpu.VMEM((2, n_sp, tokens, 2 * HEAD), bf16),
            pltpu.VMEM((2, n_sp // n_y, n_y, tokens, 2 * HEAD), bf16),
            pltpu.VMEM((max(sp_rows, tokens), 2 * HEAD), f32),
            pltpu.VMEM((2, sp_rows, 2 * HEAD), bf16),
            pltpu.VMEM((2, n_dp, w_rows, 2 * HEAD), bf16),
            sem((2, n_sp)), sem((2, n_sp)),
            sem((n_sp,)), sem((n_sp,)),
            sem((n_sp,)), sem((n_sp,)),
            sem((n_dp,)), sem((n_dp,)), sem((n_dp,)), sem((n_dp,)), sem((n_dp,)),
            sem((2, n_sp)), sem((2, n_sp)),
            sem((2, 2, n_sp)), sem((2, 2, n_sp)),
            sem((2, 2, 2)), sem((2, 2, 2)),
            sem((2, 2, 2)), sem((2, 2, 2)),
            sem((2, n_dp)), sem((2, n_dp)),
        ],
        compiler_params=pltpu.CompilerParams(
            collective_id=0, has_side_effects=True, vmem_limit_bytes=56 * 2**20
        ),
        cost_estimate=pl.CostEstimate(flops=12 * 2**30, bytes_accessed=8 * 2**20, transcendentals=8 * 2**20),
        name="attention_grads",
    )(layer_input, queries, keys, values, out_grad, key_value_weight)


def solution(mesh):
    placed = P(("dp", "sp"), None)
    return jax.shard_map(
        body,
        mesh=mesh,
        in_specs=(placed,) * 6,
        out_specs=(placed,) * 3,
        check_vma=False,
    )
```
